128 devices in a mesh: tiles: 128 (over z, x, y, core).
Axes of the slice: x: 4, y: 4, z: 4, core: 2. Of those that a mesh axis runs over, the one named last changes fastest.
Arguments:
- prognostic: float32 [128, 2, 384, 450], P('tiles'), may hold values from -6 to 6
- cutoffs: int32 [32], replicated, may hold values from 24 to 191, as said below
- listed: int32 [128, 5], P('tiles'), may hold values from -1 to 5, as said below
- weight_in: bfloat16 [384, 512], replicated, may hold values from -0.3125 to 0.3125
- weight_mid: bfloat16 [512, 512], replicated, may hold values from -0.25 to 0.25
- weight_out: bfloat16 [512, 384], replicated, may hold values from -0.25 to 0.25
Outputs:
- updated: float32 [128, 2, 384, 450], P('tiles')
The draws below stay inside these ranges and needn't reach their ends.
Inputs may be any that keep to these rules, and one draw needn't show every extreme that they name: `cutoffs`: Non-increasing along the rows; the first row holds the largest value and the last row the smallest. `listed`: row t names distinct blocks first and -1 after them; row t and row t XOR (64) name exactly 6 blocks together; some row names 5 blocks.
All inputs are finite; a program needn't handle non-finite values.
Results may differ from the reference program's by a relative error of at most 0.00094.
Values may be sent and summed in bfloat16 or wider, within the bound.
A program may use at most 192 MiB of HBM per device.

```python
import math
import jax
import jax.numpy as jnp
from jax import lax

NLON = 3600
HIDDEN_UNITS = 512
KMAX = 192
ROWS_DEV = 2
CHANNELS = 384
LSEG = 450
BLOCK_LON = 150
BLOCKS_DEV = 6
LIST_MAX = 5
ROWS = 32
N_TILES = 128


def draw_cutoffs(key, part):
    key = jax.random.fold_in(key, 5)
    values = jax.random.randint(key, (ROWS,), KMAX // 8, KMAX)
    values = jnp.sort(values)[::-1]
    values = values.at[0].set(KMAX - 1).at[ROWS - 1].set(KMAX // 8)
    return values.astype(jnp.int32)


def draw_listed(key, part):
    key = jax.random.fold_in(key, 11)
    pair_count = N_TILES // 2
    key_load, key_force, key_side, key_order = jax.random.split(key, 4)
    heavy = jax.random.randint(key_load, (pair_count,), BLOCKS_DEV // 2, LIST_MAX + 1)
    forced = jax.random.randint(key_force, (), 0, pair_count)
    heavy = jnp.where(jnp.arange(pair_count) == forced, LIST_MAX, heavy)
    flipped = jax.random.randint(key_side, (pair_count,), 0, 2)
    first_dev = jnp.arange(pair_count)
    first_load = jnp.where(flipped == 0, heavy, BLOCKS_DEV - heavy)
    loads = jnp.zeros((N_TILES,), jnp.int32)
    loads = loads.at[first_dev].set(first_load).at[first_dev + pair_count].set(BLOCKS_DEV - first_load)
    tile_keys = jax.random.split(key_order, N_TILES)
    orders = jax.vmap(lambda single: jax.random.permutation(single, BLOCKS_DEV))(tile_keys)[:, :LIST_MAX]
    slots = jnp.arange(LIST_MAX)
    return jnp.where(slots[None, :] < loads[:, None], orders, -1).astype(jnp.int32)


def levels(stream_key, shape, cuts, low, high):
    loudness = 1.0
    for dim, parts in cuts:
        draws = jax.random.uniform(jax.random.fold_in(jax.random.fold_in(stream_key, 6), dim), (parts,), jnp.float32, low / len(cuts), high / len(cuts))
        loudness = loudness * jnp.repeat(jnp.exp(draws), shape[dim] // parts).reshape((-1,) + (1,) * (len(shape) - 1 - dim))
    return loudness


def bell_draw(key, dims, scale, bound, cuts=(), kind=jnp.bfloat16):
    entries = jax.random.normal(key, dims, jnp.float32) * scale
    if len(cuts) > 0:
        entries = levels(key, dims, cuts, -0.22, 0.18) * entries
    return jnp.clip(entries, min=-bound, max=bound).astype(kind)


def setup_inputs(seed: int = 0) -> dict:
    keys = jax.random.split(jax.random.key(seed), 7)
    return {
        "prognostic": bell_draw(keys[0], (N_TILES, ROWS_DEV, CHANNELS, LSEG), 1.0, 6.0, ((0, 128),), jnp.float32),
        "cutoffs": draw_cutoffs(jax.random.fold_in(keys[6], 71), 0),
        "listed": draw_listed(jax.random.fold_in(keys[6], 71), 0),
        "weight_in": bell_draw(keys[3], (CHANNELS, HIDDEN_UNITS), CHANNELS ** -0.5, 0.3125),
        "weight_mid": bell_draw(keys[4], (HIDDEN_UNITS, HIDDEN_UNITS), HIDDEN_UNITS ** -0.5, 0.25),
        "weight_out": bell_draw(keys[5], (HIDDEN_UNITS, CHANNELS), HIDDEN_UNITS ** -0.5, 0.25),
    }


def basis_tables(length, waves):
    points = jnp.arange(length, dtype=jnp.int32)
    numbers = jnp.arange(waves, dtype=jnp.int32)
    phases = (points[:, None] * numbers[None, :]) % length
    radians = phases.astype(jnp.float32) * (2.0 * math.pi / length)
    return jnp.cos(radians), jnp.sin(radians)


def physics_net(columns, weight_in, weight_mid, weight_out):
    first = jnp.einsum("ch,scb->shb", weight_in.astype(jnp.float32), columns.astype(jnp.float32))
    first = jax.nn.silu(first).astype(jnp.bfloat16)
    second = jnp.einsum("hg,shb->sgb", weight_mid.astype(jnp.float32), first.astype(jnp.float32))
    second = jax.nn.silu(second).astype(jnp.bfloat16)
    return jnp.einsum("gc,sgb->scb", weight_out.astype(jnp.float32), second.astype(jnp.float32))


def reference(prognostic, cutoffs, listed, weight_in, weight_mid, weight_out):
    lat_count = N_TILES // 8
    grid = prognostic.reshape(8, lat_count, ROWS_DEV, CHANNELS, LSEG).transpose(1, 2, 3, 0, 4)
    grid = grid.reshape(lat_count, ROWS_DEV * CHANNELS, NLON)
    cosine, sine = basis_tables(NLON, KMAX)
    numbers = jnp.arange(KMAX, dtype=jnp.int32)
    factors = jnp.where(numbers == 0, 1.0, 2.0).astype(jnp.float32) / NLON

    def filter_tile(pieces):
        rows, limits = pieces
        coef_cos = jnp.dot(rows, cosine, precision=lax.Precision.HIGHEST, preferred_element_type=jnp.float32)
        coef_sin = jnp.dot(rows, sine, precision=lax.Precision.HIGHEST, preferred_element_type=jnp.float32)
        row_limit = jnp.repeat(limits, CHANNELS)
        scaling = jnp.where(numbers[None, :] <= row_limit[:, None], factors[None, :], 0.0)
        return (jnp.dot(coef_cos * scaling, cosine.T, precision=lax.Precision.HIGHEST, preferred_element_type=jnp.float32)
                + jnp.dot(coef_sin * scaling, sine.T, precision=lax.Precision.HIGHEST, preferred_element_type=jnp.float32))

    filtered = lax.map(filter_tile, (grid, cutoffs.reshape(lat_count, ROWS_DEV)))
    field = filtered.reshape(lat_count, ROWS_DEV, CHANNELS, 8, LSEG).transpose(3, 0, 1, 2, 4)
    field = field.reshape(N_TILES, ROWS_DEV, CHANNELS, 3, BLOCK_LON).transpose(0, 1, 3, 2, 4)
    blocks = field.reshape(N_TILES, BLOCKS_DEV, CHANNELS, BLOCK_LON)

    def tile_physics(pieces):
        tile_blocks, block_list = pieces
        picked = jnp.take(tile_blocks, jnp.clip(block_list, 0, BLOCKS_DEV - 1), axis=0).astype(jnp.bfloat16)
        tendency = physics_net(picked, weight_in, weight_mid, weight_out)
        target = jnp.where(block_list >= 0, block_list, BLOCKS_DEV).astype(jnp.int32)
        return tile_blocks.at[target].add(tendency, mode="drop")

    result = lax.map(tile_physics, (blocks, listed))
    result = result.reshape(N_TILES, ROWS_DEV, 3, CHANNELS, BLOCK_LON).transpose(0, 1, 3, 2, 4)
    return result.reshape(N_TILES, ROWS_DEV, CHANNELS, LSEG)
```

```python
import math

import jax
import jax.numpy as jnp
import ml_dtypes
import numpy as np
from jax import lax
from jax.experimental import pallas as pl
from jax.experimental.pallas import tpu as pltpu
from jax.sharding import PartitionSpec as P

NLON = 3600
KMAX = 192
SEGMENTS = 8
SEG = NLON // SEGMENTS
COEFS = 2 * KMAX
LATS = 16
ROWS = 2
CHANNELS = 384
OWNED = CHANNELS // SEGMENTS
BLOCK_LON = 150
LIST_MAX = 5
TOP = 32000.0
PARTS = ((0, 0, 48), (1, 0, 48))
MESH = pl.DeviceIdType.MESH


def tables():
    points = np.arange(NLON)[:, None]
    numbers = np.arange(KMAX)[None, :]
    radians = (points * numbers % NLON) * (2.0 * math.pi / NLON)
    both = np.concatenate([np.sin(radians), np.cos(radians)], axis=1)
    weights = np.where(np.arange(KMAX) == 0, 1.0, 2.0) / NLON
    forward = both.reshape(SEGMENTS, SEG, COEFS).transpose(0, 2, 1)
    inverse = (both * np.concatenate([weights, weights])).reshape(SEGMENTS, SEG, COEFS)

    def split_table(table):
        high = table.astype(ml_dtypes.bfloat16)
        low = (table - high.astype(np.float64)).astype(ml_dtypes.bfloat16)
        return np.stack([high, low], axis=1)

    return split_table(forward), split_table(inverse)


def split(value):
    high = value.astype(jnp.bfloat16)
    return high, (value - high.astype(jnp.float32)).astype(jnp.bfloat16)


def dot(a, b):
    return jnp.dot(a, b, preferred_element_type=jnp.float32)


def dot3(table, value):
    high, low = split(value)
    return dot(table[0], high) + (dot(table[1], high) + dot(table[0], low))


def encode(value):
    top = jnp.maximum(jnp.max(jnp.abs(value), axis=0, keepdims=True), 1e-30)
    whole = jnp.floor(value * (TOP / top) + 0.5)
    return whole.astype(jnp.int32).astype(jnp.int16), top * (1.0 / TOP)


def decode(code, scale):
    return code.astype(jnp.int32).astype(jnp.float32) * scale


def silu(v):
    return v * (0.5 + 0.5 * jnp.tanh(0.5 * v))


def kernel(
    state, cutoffs, listed, w_in, w_mid, w_out, forward, inverse, out,
    x_v, f_v, i_v, wi_v, wm_v, wo_v, part_v, part_s, got_v, got_s, sum_v, sum_s, all_v, all_s, out_v,
    load_sem, store_sem, s1, r1, s2, r2,
):
    me = lax.axis_index("tiles")
    seat = me // LATS
    lat = lax.rem(me, LATS)
    other = lax.rem(lat + LATS // 2, LATS)
    z = seat // 2
    seats = [lax.rem(z + dz, 4) * 2 + side for dz in (2, 1, 3, 0) for side in (0, 1)]

    barrier = pltpu.get_barrier_semaphore()
    for j in seats:
        pl.semaphore_signal(barrier, inc=1, device_id=(j * LATS + other,), device_id_type=MESH)

    loads = [
        pltpu.make_async_copy(src, dst, load_sem.at[i])
        for i, (src, dst) in enumerate(
            (
                (state.at[0, :, 0, :], x_v.at[0]),
                (forward.at[seat], f_v),
                (state.at[0, :, 1, :], x_v.at[1]),
                (inverse.at[seat], i_v),
                (w_in, wi_v),
                (w_mid, wm_v),
                (w_out, wo_v),
            )
        )
    ]
    for load in loads:
        load.start()

    def pair(part, slot, code, scale, code_to, scale_to, send_sem, recv_sem, j, owner):
        return [
            pltpu.make_async_remote_copy(
                src_ref=src,
                dst_ref=dst,
                send_sem=send_sem.at[what, part, slot],
                recv_sem=recv_sem.at[what, part, owner],
                device_id=(j * LATS + other,),
                device_id_type=MESH,
            )
            for what, (src, dst) in enumerate(((scale, scale_to), (code, code_to)))
        ]

    def coefs(j, first, size):
        return pl.ds(pl.multiple_of(j * OWNED + first, 16), size)

    sent = []
    for row in range(ROWS):
        if row == 0:
            loads[0].wait()
            loads[1].wait()
        else:
            loads[2].wait()
        part_v[row], part_s[row] = encode(dot3(f_v, x_v[row]))
        if row == 0:
            pl.semaphore_wait(barrier, SEGMENTS)
        for part, (at, first, size) in enumerate(PARTS):
            if at == row:
                for slot, j in enumerate(seats):
                    copies = pair(
                        part, slot,
                        part_v.at[row, coefs(j, first, size)], part_s.at[row],
                        got_v.at[seat, row, pl.ds(first, size)], got_s.at[part, seat],
                        s1, r1, j, seat,
                    )
                    for copy in copies:
                        copy.start()
                    sent += copies

    for part, (row, first, size) in enumerate(PARTS):
        total = None
        for j in range(SEGMENTS):
            code, scale = got_v.at[j, row, pl.ds(first, size)], got_s.at[part, j]
            for copy in pair(part, 0, code, scale, code, scale, s1, r1, j, j):
                copy.wait_recv()
            value = decode(code[...], scale[...])
            total = value if total is None else total + value
        number = lax.rem(seat, 4) * OWNED + first + lax.broadcasted_iota(jnp.int32, (size, 1), 0)
        total = jnp.where(number <= cutoffs[other * ROWS + row], total, 0.0)
        sum_v[row, pl.ds(first, size)], sum_s[part] = encode(total)
        for slot, j in enumerate(seats):
            copies = pair(
                part, slot,
                sum_v.at[row, pl.ds(first, size)], sum_s.at[part],
                all_v.at[row, coefs(seat, first, size)], all_s.at[part, seat],
                s2, r2, j, seat,
            )
            for copy in copies:
                copy.start()
            sent += copies

    for i in range(3, 7):
        loads[i].wait()
    point = lax.broadcasted_iota(jnp.int32, (SEG, 1), 0)
    stores = []
    for row in range(ROWS):
        pieces = {}
        for part, (at, first, size) in enumerate(PARTS):
            if at == row:
                for j in range(SEGMENTS):
                    code, scale = all_v.at[row, pl.ds(j * OWNED + first, size)], all_s.at[part, j]
                    for copy in pair(part, 0, code, scale, code, scale, s2, r2, j, j):
                        copy.wait_recv()
                    pieces[j * OWNED + first] = decode(code[...], scale[...])
        smooth = dot3(i_v, jnp.concatenate([pieces[k] for k in sorted(pieces)], axis=0))
        h = smooth.astype(jnp.bfloat16)
        h = silu(dot(h, wi_v[...])).astype(jnp.bfloat16)
        h = silu(dot(h, wm_v[...])).astype(jnp.bfloat16)
        tendency = dot(h, wo_v[...])
        block = 3 * row + jnp.where(point >= BLOCK_LON, 1, 0) + jnp.where(point >= 2 * BLOCK_LON, 1, 0)
        hit = block == listed[0, 0]
        for i in range(1, LIST_MAX):
            hit = jnp.logical_or(hit, block == listed[0, i])
        out_v[row] = smooth + jnp.where(hit, tendency, 0.0)
        store = pltpu.make_async_copy(out_v.at[row], out.at[0, :, row, :], store_sem.at[row])
        store.start()
        stores.append(store)
    for copy in sent:
        copy.wait_send()
    for store in stores:
        store.wait()


def local(forward, inverse, state, cutoffs, listed, w_in, w_mid, w_out):
    hbm = pl.BlockSpec(memory_space=pl.ANY)
    smem = pl.BlockSpec(memory_space=pltpu.SMEM)
    parts = len(PARTS)
    hidden = w_mid.shape[0]
    f32, bf16, i16 = jnp.float32, jnp.bfloat16, jnp.int16
    dma = pltpu.SemaphoreType.DMA
    result = pl.pallas_call(
        kernel,
        out_shape=jax.ShapeDtypeStruct((1, SEG, ROWS, CHANNELS), f32),
        in_specs=[hbm, smem, smem, hbm, hbm, hbm, hbm, hbm],
        out_specs=hbm,
        scratch_shapes=[
            pltpu.VMEM((ROWS, SEG, CHANNELS), f32),
            pltpu.VMEM((2, COEFS, SEG), bf16),
            pltpu.VMEM((2, SEG, COEFS), bf16),
            pltpu.VMEM((CHANNELS, hidden), bf16),
            pltpu.VMEM((hidden, hidden), bf16),
            pltpu.VMEM((hidden, CHANNELS), bf16),
            pltpu.VMEM((ROWS, COEFS, CHANNELS), i16),
            pltpu.VMEM((ROWS, 1, CHANNELS), f32),
            pltpu.VMEM((SEGMENTS, ROWS, OWNED, CHANNELS), i16),
            pltpu.VMEM((parts, SEGMENTS, 1, CHANNELS), f32),
            pltpu.VMEM((ROWS, OWNED, CHANNELS), i16),
            pltpu.VMEM((parts, 1, CHANNELS), f32),
            pltpu.VMEM((ROWS, COEFS, CHANNELS), i16),
            pltpu.VMEM((parts, SEGMENTS, 1, CHANNELS), f32),
            pltpu.VMEM((ROWS, SEG, CHANNELS), f32),
            dma((7,)),
            dma((ROWS,)),
            dma((2, parts, SEGMENTS)),
            dma((2, parts, SEGMENTS)),
            dma((2, parts, SEGMENTS)),
            dma((2, parts, SEGMENTS)),
        ],
        compiler_params=pltpu.CompilerParams(
            collective_id=0, has_side_effects=True, vmem_limit_bytes=48 << 20
        ),
        cost_estimate=pl.CostEstimate(flops=3_000_000_000, bytes_accessed=6_000_000, transcendentals=1_000_000),
    )(state.transpose(0, 3, 1, 2), cutoffs, listed, w_in, w_mid, w_out, forward, inverse)
    return result.transpose(0, 2, 3, 1)


def solution(mesh):
    forward, inverse = tables()

    def whole(prognostic, cutoffs, listed, weight_in, weight_mid, weight_out):
        return local(
            jnp.asarray(forward), jnp.asarray(inverse), prognostic, cutoffs, listed, weight_in, weight_mid, weight_out
        )

    return jax.shard_map(
        whole,
        mesh=mesh,
        in_specs=(P("tiles", None, None, None), P(), P("tiles", None), P(), P(), P()),
        out_specs=P("tiles", None, None, None),
        check_vma=False,
    )
```

```python
import math

import jax
import jax.numpy as jnp
import ml_dtypes
import numpy as np
from jax import lax
from jax.experimental import pallas as pl
from jax.experimental.pallas import tpu as pltpu
from jax.sharding import PartitionSpec as P

NLON = 3600
KMAX = 192
SEGMENTS = 8
SEG = NLON // SEGMENTS
COEFS = 2 * KMAX
LATS = 16
ROWS = 2
CHANNELS = 384
OWNED = CHANNELS // SEGMENTS
BLOCK_LON = 150
LIST_MAX = 5
TOP = 32000.0
PARTS = ((0, 0, 48), (1, 0, 48))
MESH = pl.DeviceIdType.MESH


def tables():
    points = np.arange(NLON)[:, None]
    numbers = np.arange(KMAX)[None, :]
    radians = (points * numbers % NLON) * (2.0 * math.pi / NLON)
    both = np.concatenate([np.sin(radians), np.cos(radians)], axis=1)
    weights = np.where(np.arange(KMAX) == 0, 1.0, 2.0) / NLON
    forward = both.reshape(SEGMENTS, SEG, COEFS).transpose(0, 2, 1)
    inverse = (both * np.concatenate([weights, weights])).reshape(SEGMENTS, SEG, COEFS)

    def split_table(table):
        high = table.astype(ml_dtypes.bfloat16)
        low = (table - high.astype(np.float64)).astype(ml_dtypes.bfloat16)
        return np.stack([high, low], axis=1)

    return split_table(forward), split_table(inverse)


def split(value):
    high = value.astype(jnp.bfloat16)
    return high, (value - high.astype(jnp.float32)).astype(jnp.bfloat16)


def dot(a, b):
    return jnp.dot(a, b, preferred_element_type=jnp.float32)


def dot3(table, value):
    high, low = split(value)
    return dot(table[0], high) + (dot(table[1], high) + dot(table[0], low))


def encode(value):
    top = jnp.maximum(jnp.max(jnp.abs(value), axis=0, keepdims=True), 1e-30)
    whole = jnp.floor(value * (TOP / top) + 0.5)
    return whole.astype(jnp.int32).astype(jnp.int16), top * (1.0 / TOP)


def decode(code, scale):
    return code.astype(jnp.int32).astype(jnp.float32) * scale


def silu(v):
    return v * (0.5 + 0.5 * jnp.tanh(0.5 * v))


def kernel(
    state, cutoffs_h, listed_h, w_in, w_mid, w_out, forward, inverse, out,
    cutoffs, listed, x_v, f_v, i_v, wi_v, wm_v, wo_v, part_v, part_s, got_v, got_s, sum_v, sum_s, all_v, all_s, out_v,
    load_sem, store_sem, s1, r1, s2, r2,
):
    me = lax.axis_index("tiles")
    seat = me // LATS
    lat = lax.rem(me, LATS)
    other = lax.rem(lat + LATS // 2, LATS)
    z = seat // 2
    seats = [lax.rem(z + dz, 4) * 2 + side for dz in (2, 1, 3, 0) for side in (0, 1)]

    barrier = pltpu.get_barrier_semaphore()
    for j in seats:
        pl.semaphore_signal(barrier, inc=1, device_id=(j * LATS + other,), device_id_type=MESH)

    loads = [
        pltpu.make_async_copy(src, dst, load_sem.at[i])
        for i, (src, dst) in enumerate(
            (
                (state.at[0, :, 0, :], x_v.at[0]),
                (forward.at[seat], f_v),
                (state.at[0, :, 1, :], x_v.at[1]),
                (cutoffs_h, cutoffs),
                (listed_h, listed),
                (inverse.at[seat], i_v),
                (w_in, wi_v),
                (w_mid, wm_v),
                (w_out, wo_v),
            )
        )
    ]
    for load in loads:
        load.start()

    def pair(part, slot, code, scale, code_to, scale_to, send_sem, recv_sem, j, owner):
        return [
            pltpu.make_async_remote_copy(
                src_ref=src,
                dst_ref=dst,
                send_sem=send_sem.at[what, part, slot],
                recv_sem=recv_sem.at[what, part, owner],
                device_id=(j * LATS + other,),
                device_id_type=MESH,
            )
            for what, (src, dst) in enumerate(((scale, scale_to), (code, code_to)))
        ]

    def coefs(j, first, size):
        return pl.ds(pl.multiple_of(j * OWNED + first, 16), size)

    sent = []
    for row in range(ROWS):
        if row == 0:
            loads[0].wait()
            loads[1].wait()
        else:
            loads[2].wait()
        part_v[row], part_s[row] = encode(dot3(f_v, x_v[row]))
        if row == 0:
            pl.semaphore_wait(barrier, SEGMENTS)
        for part, (at, first, size) in enumerate(PARTS):
            if at == row:
                for slot, j in enumerate(seats):
                    copies = pair(
                        part, slot,
                        part_v.at[row, coefs(j, first, size)], part_s.at[row],
                        got_v.at[seat, row, pl.ds(first, size)], got_s.at[part, seat],
                        s1, r1, j, seat,
                    )
                    for copy in copies:
                        copy.start()
                    sent += copies

    loads[3].wait()
    loads[4].wait()
    for part, (row, first, size) in enumerate(PARTS):
        total = None
        for j in range(SEGMENTS):
            code, scale = got_v.at[j, row, pl.ds(first, size)], got_s.at[part, j]
            for copy in pair(part, 0, code, scale, code, scale, s1, r1, j, j):
                copy.wait_recv()
            value = decode(code[...], scale[...])
            total = value if total is None else total + value
        number = lax.rem(seat, 4) * OWNED + first + lax.broadcasted_iota(jnp.int32, (size, 1), 0)
        total = jnp.where(number <= cutoffs[other * ROWS + row], total, 0.0)
        sum_v[row, pl.ds(first, size)], sum_s[part] = encode(total)
        for slot, j in enumerate(seats):
            copies = pair(
                part, slot,
                sum_v.at[row, pl.ds(first, size)], sum_s.at[part],
                all_v.at[row, coefs(seat, first, size)], all_s.at[part, seat],
                s2, r2, j, seat,
            )
            for copy in copies:
                copy.start()
            sent += copies

    for i in range(5, 9):
        loads[i].wait()
    point = lax.broadcasted_iota(jnp.int32, (SEG, 1), 0)
    stores = []
    for row in range(ROWS):
        pieces = {}
        for part, (at, first, size) in enumerate(PARTS):
            if at == row:
                for j in range(SEGMENTS):
                    code, scale = all_v.at[row, pl.ds(j * OWNED + first, size)], all_s.at[part, j]
                    for copy in pair(part, 0, code, scale, code, scale, s2, r2, j, j):
                        copy.wait_recv()
                    pieces[j * OWNED + first] = decode(code[...], scale[...])
        smooth = dot3(i_v, jnp.concatenate([pieces[k] for k in sorted(pieces)], axis=0))
        h = smooth.astype(jnp.bfloat16)
        h = silu(dot(h, wi_v[...])).astype(jnp.bfloat16)
        h = silu(dot(h, wm_v[...])).astype(jnp.bfloat16)
        tendency = dot(h, wo_v[...])
        block = 3 * row + jnp.where(point >= BLOCK_LON, 1, 0) + jnp.where(point >= 2 * BLOCK_LON, 1, 0)
        hit = block == listed[0, 0]
        for i in range(1, LIST_MAX):
            hit = jnp.logical_or(hit, block == listed[0, i])
        out_v[row] = smooth + jnp.where(hit, tendency, 0.0)
        store = pltpu.make_async_copy(out_v.at[row], out.at[0, :, row, :], store_sem.at[row])
        store.start()
        stores.append(store)
    for copy in sent:
        copy.wait_send()
    for store in stores:
        store.wait()


def local(forward, inverse, state, cutoffs, listed, w_in, w_mid, w_out):
    hbm = pl.BlockSpec(memory_space=pltpu.HBM)
    parts = len(PARTS)
    hidden = w_mid.shape[0]
    f32, bf16, i16 = jnp.float32, jnp.bfloat16, jnp.int16
    dma = pltpu.SemaphoreType.DMA
    result = pl.pallas_call(
        kernel,
        out_shape=pltpu.VMEM((1, SEG, ROWS, CHANNELS), f32),
        in_specs=[hbm] * 8,
        out_specs=pl.BlockSpec(memory_space=pl.ANY),
        scratch_shapes=[
            pltpu.SMEM(cutoffs.shape, jnp.int32),
            pltpu.SMEM(listed.shape, jnp.int32),
            pltpu.VMEM((ROWS, SEG, CHANNELS), f32),
            pltpu.VMEM((2, COEFS, SEG), bf16),
            pltpu.VMEM((2, SEG, COEFS), bf16),
            pltpu.VMEM((CHANNELS, hidden), bf16),
            pltpu.VMEM((hidden, hidden), bf16),
            pltpu.VMEM((hidden, CHANNELS), bf16),
            pltpu.VMEM((ROWS, COEFS, CHANNELS), i16),
            pltpu.VMEM((ROWS, 1, CHANNELS), f32),
            pltpu.VMEM((SEGMENTS, ROWS, OWNED, CHANNELS), i16),
            pltpu.VMEM((parts, SEGMENTS, 1, CHANNELS), f32),
            pltpu.VMEM((ROWS, OWNED, CHANNELS), i16),
            pltpu.VMEM((parts, 1, CHANNELS), f32),
            pltpu.VMEM((ROWS, COEFS, CHANNELS), i16),
            pltpu.VMEM((parts, SEGMENTS, 1, CHANNELS), f32),
            pltpu.VMEM((ROWS, SEG, CHANNELS), f32),
            dma((9,)),
            dma((ROWS,)),
            dma((2, parts, SEGMENTS)),
            dma((2, parts, SEGMENTS)),
            dma((2, parts, SEGMENTS)),
            dma((2, parts, SEGMENTS)),
        ],
        compiler_params=pltpu.CompilerParams(
            collective_id=0, has_side_effects=True, vmem_limit_bytes=60 << 20
        ),
        cost_estimate=pl.CostEstimate(flops=3_000_000_000, bytes_accessed=6_000_000, transcendentals=1_000_000),
    )(state.transpose(0, 3, 1, 2), cutoffs, listed, w_in, w_mid, w_out, forward, inverse)
    return result.transpose(0, 2, 3, 1)


def solution(mesh):
    forward, inverse = tables()

    def whole(prognostic, cutoffs, listed, weight_in, weight_mid, weight_out):
        return local(
            jnp.asarray(forward), jnp.asarray(inverse), prognostic, cutoffs, listed, weight_in, weight_mid, weight_out
        )

    return jax.shard_map(
        whole,
        mesh=mesh,
        in_specs=(P("tiles", None, None, None), P(), P("tiles", None), P(), P(), P()),
        out_specs=P("tiles", None, None, None),
        check_vma=False,
    )
```

```python
import math

import jax
import jax.numpy as jnp
import ml_dtypes
import numpy as np
from jax import lax
from jax.experimental import pallas as pl
from jax.experimental.pallas import tpu as pltpu
from jax.sharding import PartitionSpec as P

NLON = 3600
KMAX = 192
SEGMENTS = 8
SEG = NLON // SEGMENTS
COEFS = 2 * KMAX
LATS = 16
ROWS = 2
CHANNELS = 384
OWNED = CHANNELS // SEGMENTS
BLOCK_LON = 150
LIST_MAX = 5
TOP = 32000.0
PARTS = ((0, 0, 48), (1, 0, 48))
MESH = pl.DeviceIdType.MESH


def tables():
    points = np.arange(NLON)[:, None]
    numbers = np.arange(KMAX)[None, :]
    radians = (points * numbers % NLON) * (2.0 * math.pi / NLON)
    both = np.concatenate([np.sin(radians), np.cos(radians)], axis=1)
    weights = np.where(np.arange(KMAX) == 0, 1.0, 2.0) / NLON
    forward = both.reshape(SEGMENTS, SEG, COEFS).transpose(0, 2, 1)
    inverse = (both * np.concatenate([weights, weights])).reshape(SEGMENTS, SEG, COEFS)

    def split_table(table):
        high = table.astype(ml_dtypes.bfloat16)
        low = (table - high.astype(np.float64)).astype(ml_dtypes.bfloat16)
        return np.stack([high, low], axis=1)

    return split_table(forward), split_table(inverse)


def split(value):
    high = value.astype(jnp.bfloat16)
    return high, (value - high.astype(jnp.float32)).astype(jnp.bfloat16)


def dot(a, b):
    return jnp.dot(a, b, preferred_element_type=jnp.float32)


def dot3(table, value):
    high, low = split(value)
    return dot(table[0], high) + (dot(table[1], high) + dot(table[0], low))


def encode(value):
    top = jnp.maximum(jnp.max(jnp.abs(value), axis=0, keepdims=True), 1e-30)
    whole = jnp.floor(value * (TOP / top) + 0.5)
    return whole.astype(jnp.int32).astype(jnp.int16), top * (1.0 / TOP)


def decode(code, scale):
    return code.astype(jnp.int32).astype(jnp.float32) * scale


def silu(v):
    return v * (0.5 + 0.5 * jnp.tanh(0.5 * v))


def kernel(
    state, cutoffs_h, listed_h, w_in, w_mid, w_out, forward, inverse, out,
    cutoffs, listed, x_v, f_v, i_v, wi_v, wm_v, wo_v, part_v, part_s, got_v, got_s, sum_v, sum_s, all_v, all_s,
    load_sem, s1, r1, s2, r2,
):
    me = lax.axis_index("tiles")
    seat = me // LATS
    lat = lax.rem(me, LATS)
    other = lax.rem(lat + LATS // 2, LATS)
    z = seat // 2
    seats = [lax.rem(z + dz, 4) * 2 + side for dz in (2, 1, 3, 0) for side in (0, 1)]

    barrier = pltpu.get_barrier_semaphore()
    for j in seats:
        pl.semaphore_signal(barrier, inc=1, device_id=(j * LATS + other,), device_id_type=MESH)

    loads = [
        pltpu.make_async_copy(src, dst, load_sem.at[i])
        for i, (src, dst) in enumerate(
            (
                (state.at[0, :, 0, :], x_v.at[0]),
                (forward.at[seat], f_v),
                (state.at[0, :, 1, :], x_v.at[1]),
                (cutoffs_h, cutoffs),
                (listed_h, listed),
                (inverse.at[seat], i_v),
                (w_in, wi_v),
                (w_mid, wm_v),
                (w_out, wo_v),
            )
        )
    ]
    for load in loads:
        load.start()

    def pair(part, slot, code, scale, code_to, scale_to, send_sem, recv_sem, j, owner):
        return [
            pltpu.make_async_remote_copy(
                src_ref=src,
                dst_ref=dst,
                send_sem=send_sem.at[what, part, slot],
                recv_sem=recv_sem.at[what, part, owner],
                device_id=(j * LATS + other,),
                device_id_type=MESH,
            )
            for what, (src, dst) in enumerate(((scale, scale_to), (code, code_to)))
        ]

    def coefs(j, first, size):
        return pl.ds(pl.multiple_of(j * OWNED + first, 16), size)

    sent = []
    for row in range(ROWS):
        if row == 0:
            loads[0].wait()
            loads[1].wait()
        else:
            loads[2].wait()
        part_v[row], part_s[row] = encode(dot3(f_v, x_v[row]))
        if row == 0:
            pl.semaphore_wait(barrier, SEGMENTS)
        for part, (at, first, size) in enumerate(PARTS):
            if at == row:
                for slot, j in enumerate(seats):
                    copies = pair(
                        part, slot,
                        part_v.at[row, coefs(j, first, size)], part_s.at[row],
                        got_v.at[seat, row, pl.ds(first, size)], got_s.at[part, seat],
                        s1, r1, j, seat,
                    )
                    for copy in copies:
                        copy.start()
                    sent += copies

    loads[3].wait()
    loads[4].wait()
    for part, (row, first, size) in enumerate(PARTS):
        total = None
        for j in range(SEGMENTS):
            code, scale = got_v.at[j, row, pl.ds(first, size)], got_s.at[part, j]
            for copy in pair(part, 0, code, scale, code, scale, s1, r1, j, j):
                copy.wait_recv()
            value = decode(code[...], scale[...])
            total = value if total is None else total + value
        number = lax.rem(seat, 4) * OWNED + first + lax.broadcasted_iota(jnp.int32, (size, 1), 0)
        total = jnp.where(number <= cutoffs[other * ROWS + row], total, 0.0)
        sum_v[row, pl.ds(first, size)], sum_s[part] = encode(total)
        for slot, j in enumerate(seats):
            copies = pair(
                part, slot,
                sum_v.at[row, pl.ds(first, size)], sum_s.at[part],
                all_v.at[row, coefs(seat, first, size)], all_s.at[part, seat],
                s2, r2, j, seat,
            )
            for copy in copies:
                copy.start()
            sent += copies

    for i in range(5, 9):
        loads[i].wait()
    point = lax.broadcasted_iota(jnp.int32, (SEG, 1), 0)
    for row in range(ROWS):
        pieces = {}
        for part, (at, first, size) in enumerate(PARTS):
            if at == row:
                for j in range(SEGMENTS):
                    code, scale = all_v.at[row, pl.ds(j * OWNED + first, size)], all_s.at[part, j]
                    for copy in pair(part, 0, code, scale, code, scale, s2, r2, j, j):
                        copy.wait_recv()
                    pieces[j * OWNED + first] = decode(code[...], scale[...])
        smooth = dot3(i_v, jnp.concatenate([pieces[k] for k in sorted(pieces)], axis=0))
        h = smooth.astype(jnp.bfloat16)
        h = silu(dot(h, wi_v[...])).astype(jnp.bfloat16)
        h = silu(dot(h, wm_v[...])).astype(jnp.bfloat16)
        tendency = dot(h, wo_v[...])
        block = 3 * row + jnp.where(point >= BLOCK_LON, 1, 0) + jnp.where(point >= 2 * BLOCK_LON, 1, 0)
        hit = block == listed[0, 0]
        for i in range(1, LIST_MAX):
            hit = jnp.logical_or(hit, block == listed[0, i])
        out[row] = smooth + jnp.where(hit, tendency, 0.0)
    for copy in sent:
        copy.wait_send()


def place(rows, out, sem):
    stores = [pltpu.make_async_copy(rows.at[row], out.at[0, :, row, :], sem.at[row]) for row in range(ROWS)]
    for store in stores:
        store.start()
    for store in stores:
        store.wait()


def local(forward, inverse, state, cutoffs, listed, w_in, w_mid, w_out):
    hbm = pl.BlockSpec(memory_space=pltpu.HBM)
    parts = len(PARTS)
    hidden = w_mid.shape[0]
    f32, bf16, i16 = jnp.float32, jnp.bfloat16, jnp.int16
    dma = pltpu.SemaphoreType.DMA
    result = pl.pallas_call(
        kernel,
        out_shape=pltpu.VMEM((ROWS, SEG, CHANNELS), f32),
        in_specs=[hbm] * 8,
        out_specs=pl.BlockSpec(memory_space=pltpu.VMEM),
        scratch_shapes=[
            pltpu.SMEM(cutoffs.shape, jnp.int32),
            pltpu.SMEM(listed.shape, jnp.int32),
            pltpu.VMEM((ROWS, SEG, CHANNELS), f32),
            pltpu.VMEM((2, COEFS, SEG), bf16),
            pltpu.VMEM((2, SEG, COEFS), bf16),
            pltpu.VMEM((CHANNELS, hidden), bf16),
            pltpu.VMEM((hidden, hidden), bf16),
            pltpu.VMEM((hidden, CHANNELS), bf16),
            pltpu.VMEM((ROWS, COEFS, CHANNELS), i16),
            pltpu.VMEM((ROWS, 1, CHANNELS), f32),
            pltpu.VMEM((SEGMENTS, ROWS, OWNED, CHANNELS), i16),
            pltpu.VMEM((parts, SEGMENTS, 1, CHANNELS), f32),
            pltpu.VMEM((ROWS, OWNED, CHANNELS), i16),
            pltpu.VMEM((parts, 1, CHANNELS), f32),
            pltpu.VMEM((ROWS, COEFS, CHANNELS), i16),
            pltpu.VMEM((parts, SEGMENTS, 1, CHANNELS), f32),
            dma((9,)),
            dma((2, parts, SEGMENTS)),
            dma((2, parts, SEGMENTS)),
            dma((2, parts, SEGMENTS)),
            dma((2, parts, SEGMENTS)),
        ],
        compiler_params=pltpu.CompilerParams(
            collective_id=0, has_side_effects=True, vmem_limit_bytes=60 << 20
        ),
        cost_estimate=pl.CostEstimate(flops=3_000_000_000, bytes_accessed=6_000_000, transcendentals=1_000_000),
    )(state.transpose(0, 3, 1, 2), cutoffs, listed, w_in, w_mid, w_out, forward, inverse)
    result = pl.pallas_call(
        place,
        out_shape=jax.ShapeDtypeStruct((1, SEG, ROWS, CHANNELS), f32),
        in_specs=[pl.BlockSpec(memory_space=pltpu.VMEM)],
        out_specs=hbm,
        scratch_shapes=[dma((ROWS,))],
    )(pltpu.with_memory_space_constraint(result, pltpu.VMEM))
    return result.transpose(0, 2, 3, 1)


def solution(mesh):
    forward, inverse = tables()

    def whole(prognostic, cutoffs, listed, weight_in, weight_mid, weight_out):
        return local(
            jnp.asarray(forward), jnp.asarray(inverse), prognostic, cutoffs, listed, weight_in, weight_mid, weight_out
        )

    return jax.shard_map(
        whole,
        mesh=mesh,
        in_specs=(P("tiles", None, None, None), P(), P("tiles", None), P(), P(), P()),
        out_specs=P("tiles", None, None, None),
        check_vma=False,
    )
```

```python
import math

import jax
import jax.numpy as jnp
import ml_dtypes
import numpy as np
from jax import lax
from jax.experimental import pallas as pl
from jax.experimental.pallas import tpu as pltpu
from jax.sharding import PartitionSpec as P

NLON = 3600
KMAX = 192
SEGMENTS = 8
SEG = NLON // SEGMENTS
COEFS = 2 * KMAX
LATS = 16
ROWS = 2
CHANNELS = 384
OWNED = CHANNELS // SEGMENTS
BLOCK_LON = 150
LIST_MAX = 5
TOP = 32000.0
MESH = pl.DeviceIdType.MESH


def tables():
    points = np.arange(NLON)[:, None]
    numbers = np.arange(KMAX)[None, :]
    radians = (points * numbers % NLON) * (2.0 * math.pi / NLON)
    both = np.concatenate([np.sin(radians), np.cos(radians)], axis=1)
    weights = np.where(np.arange(KMAX) == 0, 1.0, 2.0) / NLON
    forward = both.reshape(SEGMENTS, SEG, COEFS).transpose(0, 2, 1)
    inverse = (both * np.concatenate([weights, weights])).reshape(SEGMENTS, SEG, COEFS)

    def split_table(table):
        high = table.astype(ml_dtypes.bfloat16)
        low = (table - high.astype(np.float64)).astype(ml_dtypes.bfloat16)
        return np.stack([high, low], axis=1)

    return split_table(forward), split_table(inverse)


def split(value):
    high = value.astype(jnp.bfloat16)
    return high, (value - high.astype(jnp.float32)).astype(jnp.bfloat16)


def dot(a, b):
    return jnp.dot(a, b, preferred_element_type=jnp.float32)


def dot3(table, value):
    high, low = split(value)
    return dot(table[0], high) + (dot(table[1], high) + dot(table[0], low))


def encode(value):
    top = jnp.maximum(jnp.max(jnp.abs(value), axis=0, keepdims=True), 1e-30)
    whole = jnp.floor(value * (TOP / top) + 0.5)
    return whole.astype(jnp.int32).astype(jnp.int16), top * (1.0 / TOP)


def decode(code, scale):
    return code.astype(jnp.int32).astype(jnp.float32) * scale


def silu_of_half(u):
    return u + u * jnp.tanh(u)


def kernel(
    state, cutoffs_h, listed_h, w_in, w_mid, w_out, forward, inverse, out,
    cutoffs, listed, x_v, f_v, i_v, wi_v, wm_v, wo_v, part_v, part_s, got_v, got_s, sum_v, sum_s, all_v, all_s,
    load_sem, s1, r1, s2, r2,
):
    me = lax.axis_index("tiles")
    seat = me // LATS
    lat = lax.rem(me, LATS)
    other = lax.rem(lat + LATS // 2, LATS)
    z = seat // 2
    seats = [
        lax.rem(z + dz, 4) * 2 + side
        for dz, side in ((2, 0), (2, 1), (1, 0), (3, 1), (1, 1), (3, 0), (0, 0), (0, 1))
    ]

    barrier = pltpu.get_barrier_semaphore()
    for j in seats:
        pl.semaphore_signal(barrier, inc=1, device_id=(j * LATS + other,), device_id_type=MESH)

    loads = [
        pltpu.make_async_copy(src, dst, load_sem.at[i])
        for i, (src, dst) in enumerate(
            (
                (state.at[0, :, 0, :], x_v.at[0]),
                (forward.at[seat], f_v),
                (state.at[0, :, 1, :], x_v.at[1]),
                (cutoffs_h, cutoffs),
                (listed_h, listed),
                (inverse.at[seat], i_v),
                (w_in, wi_v),
                (w_mid, wm_v),
                (w_out, wo_v),
            )
        )
    ]
    for load in loads:
        load.start()

    def move(row, code, scale, code_to, scale_to, send_sem, recv_sem, j):
        return [
            pltpu.make_async_remote_copy(
                src_ref=src,
                dst_ref=dst,
                send_sem=send_sem.at[what, row],
                recv_sem=recv_sem.at[what, row],
                device_id=(j * LATS + other,),
                device_id_type=MESH,
            )
            for what, (src, dst) in enumerate(((scale, scale_to), (code, code_to)))
        ]

    def owned(j):
        return pl.ds(pl.multiple_of(j * OWNED, 16), OWNED)

    def all_copies(row, code, scale, send_sem, recv_sem):
        return move(row, code, scale, code, scale, send_sem, recv_sem, seats[0])

    for row in range(ROWS):
        if row == 0:
            loads[0].wait()
            loads[1].wait()
        else:
            loads[2].wait()
        part_v[row], part_s[row] = encode(dot3(f_v, x_v[row]))
        if row == 0:
            pl.semaphore_wait(barrier, SEGMENTS)
        for j in seats:
            for copy in move(
                row, part_v.at[row, owned(j)], part_s.at[row], got_v.at[row, seat], got_s.at[row, seat], s1, r1, j
            ):
                copy.start()

    for i in range(3, 9):
        loads[i].wait()
    wi_v[...] = wi_v[...] * jnp.bfloat16(0.5)
    wm_v[...] = wm_v[...] * jnp.bfloat16(0.5)
    for row in range(ROWS):
        for copies in all_copies(row, got_v.at[row], got_s.at[row], s1, r1):
            copies.wait_recv()
        total = decode(got_v[row, 0], got_s[row, 0])
        for j in range(1, SEGMENTS):
            total = total + decode(got_v[row, j], got_s[row, j])
        number = lax.rem(seat, 4) * OWNED + lax.broadcasted_iota(jnp.int32, (OWNED, 1), 0)
        total = jnp.where(number <= cutoffs[other * ROWS + row], total, 0.0)
        sum_v[row], sum_s[row] = encode(total)
        for j in seats:
            for copy in move(
                row, sum_v.at[row], sum_s.at[row], all_v.at[row, owned(seat)], all_s.at[row, seat], s2, r2, j
            ):
                copy.start()

    point = lax.broadcasted_iota(jnp.int32, (SEG, 1), 0)
    for row in range(ROWS):
        if row > 0:
            for back in range(ROWS):
                for copies in all_copies(back, part_v.at[back], got_s.at[back], s1, r1):
                    copies.wait_send()
                for copies in all_copies(back, all_v.at[back], all_s.at[back], s2, r2):
                    copies.wait_send()
        for copies in all_copies(row, all_v.at[row], all_s.at[row], s2, r2):
            copies.wait_recv()
        coefs = jnp.concatenate(
            [decode(all_v[row, pl.ds(j * OWNED, OWNED)], all_s[row, j]) for j in range(SEGMENTS)], axis=0
        )
        high, low = split(coefs)
        smooth = dot(i_v[0], high) + (dot(i_v[1], high) + dot(i_v[0], low))
        h = smooth.astype(jnp.bfloat16)
        h = silu_of_half(dot(h, wi_v[...])).astype(jnp.bfloat16)
        h = silu_of_half(dot(h, wm_v[...])).astype(jnp.bfloat16)
        tendency = dot(h, wo_v[...])
        block = 3 * row + jnp.where(point >= BLOCK_LON, 1, 0) + jnp.where(point >= 2 * BLOCK_LON, 1, 0)
        hit = block == listed[0, 0]
        for i in range(1, LIST_MAX):
            hit = jnp.logical_or(hit, block == listed[0, i])
        out[row] = smooth + jnp.where(hit, tendency, 0.0)


def place(rows, out, sem):
    stores = [pltpu.make_async_copy(rows.at[row], out.at[0, :, row, :], sem.at[row]) for row in range(ROWS)]
    for store in stores:
        store.start()
    for store in stores:
        store.wait()


def local(forward, inverse, state, cutoffs, listed, w_in, w_mid, w_out):
    hbm = pl.BlockSpec(memory_space=pltpu.HBM)
    hidden = w_mid.shape[0]
    f32, bf16, i16 = jnp.float32, jnp.bfloat16, jnp.int16
    dma = pltpu.SemaphoreType.DMA
    result = pl.pallas_call(
        kernel,
        out_shape=pltpu.VMEM((ROWS, SEG, CHANNELS), f32),
        in_specs=[hbm] * 8,
        out_specs=pl.BlockSpec(memory_space=pltpu.VMEM),
        scratch_shapes=[
            pltpu.SMEM(cutoffs.shape, jnp.int32),
            pltpu.SMEM(listed.shape, jnp.int32),
            pltpu.VMEM((ROWS, SEG, CHANNELS), f32),
            pltpu.VMEM((2, COEFS, SEG), bf16),
            pltpu.VMEM((2, SEG, COEFS), bf16),
            pltpu.VMEM((CHANNELS, hidden), bf16),
            pltpu.VMEM((hidden, hidden), bf16),
            pltpu.VMEM((hidden, CHANNELS), bf16),
            pltpu.VMEM((ROWS, COEFS, CHANNELS), i16),
            pltpu.VMEM((ROWS, 1, CHANNELS), f32),
            pltpu.VMEM((ROWS, SEGMENTS, OWNED, CHANNELS), i16),
            pltpu.VMEM((ROWS, SEGMENTS, 1, CHANNELS), f32),
            pltpu.VMEM((ROWS, OWNED, CHANNELS), i16),
            pltpu.VMEM((ROWS, 1, CHANNELS), f32),
            pltpu.VMEM((ROWS, COEFS, CHANNELS), i16),
            pltpu.VMEM((ROWS, SEGMENTS, 1, CHANNELS), f32),
            dma((9,)),
            dma((2, ROWS)),
            dma((2, ROWS)),
            dma((2, ROWS)),
            dma((2, ROWS)),
        ],
        compiler_params=pltpu.CompilerParams(
            collective_id=0, has_side_effects=True, vmem_limit_bytes=60 << 20
        ),
        cost_estimate=pl.CostEstimate(flops=3_000_000_000, bytes_accessed=6_000_000, transcendentals=1_000_000),
    )(state.transpose(0, 3, 1, 2), cutoffs, listed, w_in, w_mid, w_out, forward, inverse)
    result = pl.pallas_call(
        place,
        out_shape=jax.ShapeDtypeStruct((1, SEG, ROWS, CHANNELS), f32),
        in_specs=[pl.BlockSpec(memory_space=pltpu.VMEM)],
        out_specs=hbm,
        scratch_shapes=[dma((ROWS,))],
    )(pltpu.with_memory_space_constraint(result, pltpu.VMEM))
    return result.transpose(0, 2, 3, 1)


def solution(mesh):
    forward, inverse = tables()

    def whole(prognostic, cutoffs, listed, weight_in, weight_mid, weight_out):
        return local(
            jnp.asarray(forward), jnp.asarray(inverse), prognostic, cutoffs, listed, weight_in, weight_mid, weight_out
        )

    return jax.shard_map(
        whole,
        mesh=mesh,
        in_specs=(P("tiles", None, None, None), P(), P("tiles", None), P(), P(), P()),
        out_specs=P("tiles", None, None, None),
        check_vma=False,
    )
```

```python
import math

import jax
import jax.numpy as jnp
import ml_dtypes
import numpy as np
from jax import lax
from jax.experimental import pallas as pl
from jax.experimental.pallas import tpu as pltpu
from jax.sharding import PartitionSpec as P

NLON = 3600
KMAX = 192
SEGMENTS = 8
SEG = NLON // SEGMENTS
COEFS = 2 * KMAX
LATS = 16
ROWS = 2
CHANNELS = 384
OWNED = CHANNELS // SEGMENTS
BLOCK_LON = 150
LIST_MAX = 5
TOP = 32000.0
MESH = pl.DeviceIdType.MESH


def tables():
    points = np.arange(NLON)[:, None]
    numbers = np.arange(KMAX)[None, :]
    radians = (points * numbers % NLON) * (2.0 * math.pi / NLON)
    both = np.concatenate([np.sin(radians), np.cos(radians)], axis=1)
    weights = np.where(np.arange(KMAX) == 0, 1.0, 2.0) / NLON
    forward = both.reshape(SEGMENTS, SEG, COEFS).transpose(0, 2, 1)
    inverse = (both * np.concatenate([weights, weights])).reshape(SEGMENTS, SEG, COEFS)

    def split_table(table):
        high = table.astype(ml_dtypes.bfloat16)
        low = (table - high.astype(np.float64)).astype(ml_dtypes.bfloat16)
        return np.stack([high, low], axis=1)

    high, low = split_table(inverse).swapaxes(0, 1)
    return split_table(forward), np.concatenate([high, low, high], axis=2)


def split(value):
    high = value.astype(jnp.bfloat16)
    return high, (value - high.astype(jnp.float32)).astype(jnp.bfloat16)


def dot(a, b):
    return jnp.dot(a, b, preferred_element_type=jnp.float32)


def dot3(table, value):
    high, low = split(value)
    return dot(table[0], high) + (dot(table[1], high) + dot(table[0], low))


def encode(value):
    top = jnp.maximum(jnp.max(jnp.abs(value), axis=0, keepdims=True), 1e-30)
    whole = jnp.floor(value * (TOP / top) + 0.5)
    return whole.astype(jnp.int32).astype(jnp.int16), top * (1.0 / TOP)


def decode(code, scale):
    return code.astype(jnp.int32).astype(jnp.float32) * scale


def silu_of_half(u):
    return u + u * jnp.tanh(u)


def kernel(
    state, cutoffs_h, listed_h, w_in, w_mid, w_out, forward, inverse, out,
    cutoffs, listed, x_v, f_v, i_v, wi_v, wm_v, wo_v, part_v, part_s, got_v, got_s, sum_v, sum_s, all_v, all_s,
    load_sem, s1, r1, s2, r2,
):
    me = lax.axis_index("tiles")
    seat = me // LATS
    lat = lax.rem(me, LATS)
    other = lax.rem(lat + LATS // 2, LATS)
    z = seat // 2
    seats = [
        lax.rem(z + dz, 4) * 2 + side
        for dz, side in ((2, 0), (2, 1), (1, 0), (3, 1), (1, 1), (3, 0), (0, 0), (0, 1))
    ]

    barrier = pltpu.get_barrier_semaphore()
    for j in seats:
        pl.semaphore_signal(barrier, inc=1, device_id=(j * LATS + other,), device_id_type=MESH)

    loads = [
        pltpu.make_async_copy(src, dst, load_sem.at[i])
        for i, (src, dst) in enumerate(
            (
                (state.at[0, :, 0, :], x_v.at[0]),
                (forward.at[seat], f_v),
                (state.at[0, :, 1, :], x_v.at[1]),
                (cutoffs_h, cutoffs),
                (listed_h, listed),
                (inverse.at[seat], i_v),
                (w_in, wi_v),
                (w_mid, wm_v),
                (w_out, wo_v),
            )
        )
    ]
    for load in loads:
        load.start()

    def move(row, code, scale, code_to, scale_to, send_sem, recv_sem, j):
        return [
            pltpu.make_async_remote_copy(
                src_ref=src,
                dst_ref=dst,
                send_sem=send_sem.at[what, row],
                recv_sem=recv_sem.at[what, row],
                device_id=(j * LATS + other,),
                device_id_type=MESH,
            )
            for what, (src, dst) in enumerate(((scale, scale_to), (code, code_to)))
        ]

    def owned(j):
        return pl.ds(pl.multiple_of(j * OWNED, 16), OWNED)

    def all_copies(row, code, scale, send_sem, recv_sem):
        return move(row, code, scale, code, scale, send_sem, recv_sem, seats[0])

    for row in range(ROWS):
        if row == 0:
            loads[0].wait()
            loads[1].wait()
        else:
            loads[2].wait()
        part_v[row], part_s[row] = encode(dot3(f_v, x_v[row]))
        if row == 0:
            pl.semaphore_wait(barrier, SEGMENTS)
        for j in seats:
            for copy in move(
                row, part_v.at[row, owned(j)], part_s.at[row], got_v.at[row, seat], got_s.at[row, seat], s1, r1, j
            ):
                copy.start()

    for i in range(3, 9):
        loads[i].wait()
    wi_v[...] = wi_v[...] * jnp.bfloat16(0.5)
    wm_v[...] = wm_v[...] * jnp.bfloat16(0.5)
    for row in range(ROWS):
        for copies in all_copies(row, got_v.at[row], got_s.at[row], s1, r1):
            copies.wait_recv()
        total = decode(got_v[row, 0], got_s[row, 0])
        for j in range(1, SEGMENTS):
            total = total + decode(got_v[row, j], got_s[row, j])
        number = lax.rem(seat, 4) * OWNED + lax.broadcasted_iota(jnp.int32, (OWNED, 1), 0)
        total = jnp.where(number <= cutoffs[other * ROWS + row], total, 0.0)
        sum_v[row], sum_s[row] = encode(total)
        for j in seats:
            for copy in move(
                row, sum_v.at[row], sum_s.at[row], all_v.at[row, owned(seat)], all_s.at[row, seat], s2, r2, j
            ):
                copy.start()

    point = lax.broadcasted_iota(jnp.int32, (SEG, 1), 0)
    for row in range(ROWS):
        if row > 0:
            for back in range(ROWS):
                for copies in all_copies(back, part_v.at[back], got_s.at[back], s1, r1):
                    copies.wait_send()
                for copies in all_copies(back, all_v.at[back], all_s.at[back], s2, r2):
                    copies.wait_send()
        for copies in all_copies(row, all_v.at[row], all_s.at[row], s2, r2):
            copies.wait_recv()
        coefs = jnp.concatenate(
            [decode(all_v[row, pl.ds(j * OWNED, OWNED)], all_s[row, j]) for j in range(SEGMENTS)], axis=0
        )
        high, low = split(coefs)
        smooth = dot(i_v[...], jnp.concatenate([high, high, low], axis=0))
        h = smooth.astype(jnp.bfloat16)
        h = silu_of_half(dot(h, wi_v[...])).astype(jnp.bfloat16)
        h = silu_of_half(dot(h, wm_v[...])).astype(jnp.bfloat16)
        tendency = dot(h, wo_v[...])
        block = 3 * row + jnp.where(point >= BLOCK_LON, 1, 0) + jnp.where(point >= 2 * BLOCK_LON, 1, 0)
        hit = block == listed[0, 0]
        for i in range(1, LIST_MAX):
            hit = jnp.logical_or(hit, block == listed[0, i])
        out[row] = smooth + jnp.where(hit, tendency, 0.0)


def place(rows, out, sem):
    stores = [pltpu.make_async_copy(rows.at[row], out.at[0, :, row, :], sem.at[row]) for row in range(ROWS)]
    for store in stores:
        store.start()
    for store in stores:
        store.wait()


def local(forward, inverse, state, cutoffs, listed, w_in, w_mid, w_out):
    hbm = pl.BlockSpec(memory_space=pltpu.HBM)
    hidden = w_mid.shape[0]
    f32, bf16, i16 = jnp.float32, jnp.bfloat16, jnp.int16
    dma = pltpu.SemaphoreType.DMA
    result = pl.pallas_call(
        kernel,
        out_shape=pltpu.VMEM((ROWS, SEG, CHANNELS), f32),
        in_specs=[hbm] * 8,
        out_specs=pl.BlockSpec(memory_space=pltpu.VMEM),
        scratch_shapes=[
            pltpu.SMEM(cutoffs.shape, jnp.int32),
            pltpu.SMEM(listed.shape, jnp.int32),
            pltpu.VMEM((ROWS, SEG, CHANNELS), f32),
            pltpu.VMEM((2, COEFS, SEG), bf16),
            pltpu.VMEM((SEG, 3 * COEFS), bf16),
            pltpu.VMEM((CHANNELS, hidden), bf16),
            pltpu.VMEM((hidden, hidden), bf16),
            pltpu.VMEM((hidden, CHANNELS), bf16),
            pltpu.VMEM((ROWS, COEFS, CHANNELS), i16),
            pltpu.VMEM((ROWS, 1, CHANNELS), f32),
            pltpu.VMEM((ROWS, SEGMENTS, OWNED, CHANNELS), i16),
            pltpu.VMEM((ROWS, SEGMENTS, 1, CHANNELS), f32),
            pltpu.VMEM((ROWS, OWNED, CHANNELS), i16),
            pltpu.VMEM((ROWS, 1, CHANNELS), f32),
            pltpu.VMEM((ROWS, COEFS, CHANNELS), i16),
            pltpu.VMEM((ROWS, SEGMENTS, 1, CHANNELS), f32),
            dma((9,)),
            dma((2, ROWS)),
            dma((2, ROWS)),
            dma((2, ROWS)),
            dma((2, ROWS)),
        ],
        compiler_params=pltpu.CompilerParams(
            collective_id=0, has_side_effects=True, vmem_limit_bytes=60 << 20
        ),
        cost_estimate=pl.CostEstimate(flops=3_000_000_000, bytes_accessed=6_000_000, transcendentals=1_000_000),
    )(state.transpose(0, 3, 1, 2), cutoffs, listed, w_in, w_mid, w_out, forward, inverse)
    result = pl.pallas_call(
        place,
        out_shape=jax.ShapeDtypeStruct((1, SEG, ROWS, CHANNELS), f32),
        in_specs=[pl.BlockSpec(memory_space=pltpu.VMEM)],
        out_specs=hbm,
        scratch_shapes=[dma((ROWS,))],
    )(pltpu.with_memory_space_constraint(result, pltpu.VMEM))
    return result.transpose(0, 2, 3, 1)


def solution(mesh):
    forward, inverse = tables()

    def whole(prognostic, cutoffs, listed, weight_in, weight_mid, weight_out):
        return local(
            jnp.asarray(forward), jnp.asarray(inverse), prognostic, cutoffs, listed, weight_in, weight_mid, weight_out
        )

    return jax.shard_map(
        whole,
        mesh=mesh,
        in_specs=(P("tiles", None, None, None), P(), P("tiles", None), P(), P(), P()),
        out_specs=P("tiles", None, None, None),
        check_vma=False,
    )
```

```python
import math

import jax
import jax.numpy as jnp
import ml_dtypes
import numpy as np
from jax import lax
from jax.experimental import pallas as pl
from jax.experimental.pallas import tpu as pltpu
from jax.sharding import PartitionSpec as P

NLON = 3600
KMAX = 192
SEGMENTS = 8
SEG = NLON // SEGMENTS
COEFS = 2 * KMAX
LATS = 16
ROWS = 2
CHANNELS = 384
OWNED = CHANNELS // SEGMENTS
BLOCK_LON = 150
LIST_MAX = 5
TOP = 32000.0
MESH = pl.DeviceIdType.MESH


def tables():
    points = np.arange(NLON)[:, None]
    numbers = np.arange(KMAX)[None, :]
    radians = (points * numbers % NLON) * (2.0 * math.pi / NLON)
    both = np.concatenate([np.sin(radians), np.cos(radians)], axis=1)
    weights = np.where(np.arange(KMAX) == 0, 1.0, 2.0) / NLON
    forward = both.reshape(SEGMENTS, SEG, COEFS).transpose(0, 2, 1)
    inverse = (both * np.concatenate([weights, weights])).reshape(SEGMENTS, SEG, COEFS)

    def split_table(table):
        high = table.astype(ml_dtypes.bfloat16)
        low = (table - high.astype(np.float64)).astype(ml_dtypes.bfloat16)
        return np.stack([high, low], axis=1)

    high, low = split_table(inverse).swapaxes(0, 1)
    return split_table(forward), np.concatenate([high, low, high], axis=2)


def split(value):
    high = value.astype(jnp.bfloat16)
    return high, (value - high.astype(jnp.float32)).astype(jnp.bfloat16)


def dot(a, b):
    return jnp.dot(a, b, preferred_element_type=jnp.float32)


def dot3(table, value):
    high, low = split(value)
    return dot(table[0], high) + (dot(table[1], high) + dot(table[0], low))


def encode(value):
    top = jnp.maximum(jnp.max(jnp.abs(value), axis=0, keepdims=True), 1e-30)
    whole = jnp.floor(value * (TOP / top) + 0.5)
    return whole.astype(jnp.int32).astype(jnp.int16), top * (1.0 / TOP)


def decode(code, scale):
    return code.astype(jnp.int32).astype(jnp.float32) * scale


def silu_of_half(u):
    return u + u * jnp.tanh(u)


def finish(row, codes, scales, table, w_in, w_mid, w_out, listed, ready=None):
    coefs = jnp.concatenate([decode(codes[pl.ds(j * OWNED, OWNED)], scales[j]) for j in range(SEGMENTS)], axis=0)
    high, low = split(coefs)
    smooth = dot(table[...], jnp.concatenate([high, high, low], axis=0))
    h = smooth.astype(jnp.bfloat16)
    h = silu_of_half(dot(h, w_in[...])).astype(jnp.bfloat16)
    h = silu_of_half(dot(h, w_mid[...])).astype(jnp.bfloat16)
    tendency = dot(h, w_out[...])
    if ready is not None:
        ready()
    point = lax.broadcasted_iota(jnp.int32, (SEG, 1), 0)
    block = 3 * row + jnp.where(point >= BLOCK_LON, 1, 0) + jnp.where(point >= 2 * BLOCK_LON, 1, 0)
    hit = block == listed[0, 0]
    for i in range(1, LIST_MAX):
        hit = jnp.logical_or(hit, block == listed[0, i])
    return smooth + jnp.where(hit, tendency, 0.0)


def kernel(
    state, cutoffs_h, listed_h, w_in, w_mid, w_out, forward, inverse,
    out, code_v, scale_v, i_v, wi_v, wm_v, wo_v,
    cutoffs, listed, x_v, f_v, part_v, part_s, got_v, got_s, sum_v, sum_s, all_v, all_s,
    load_sem, s1, r1, s2, r2,
):
    me = lax.axis_index("tiles")
    seat = me // LATS
    codes, scales = (all_v, code_v), (all_s, scale_v)
    lat = lax.rem(me, LATS)
    other = lax.rem(lat + LATS // 2, LATS)
    z = seat // 2
    seats = [
        lax.rem(z + dz, 4) * 2 + side
        for dz, side in ((2, 0), (2, 1), (1, 0), (3, 1), (1, 1), (3, 0), (0, 0), (0, 1))
    ]

    barrier = pltpu.get_barrier_semaphore()
    for j in seats:
        pl.semaphore_signal(barrier, inc=1, device_id=(j * LATS + other,), device_id_type=MESH)

    loads = [
        pltpu.make_async_copy(src, dst, load_sem.at[i])
        for i, (src, dst) in enumerate(
            (
                (state.at[0, :, 0, :], x_v.at[0]),
                (forward.at[seat], f_v),
                (state.at[0, :, 1, :], x_v.at[1]),
                (cutoffs_h, cutoffs),
                (listed_h, listed),
                (inverse.at[seat], i_v),
                (w_in, wi_v),
                (w_mid, wm_v),
                (w_out, wo_v),
            )
        )
    ]
    for load in loads:
        load.start()

    def move(row, code, scale, code_to, scale_to, send_sem, recv_sem, j):
        return [
            pltpu.make_async_remote_copy(
                src_ref=src,
                dst_ref=dst,
                send_sem=send_sem.at[what, row],
                recv_sem=recv_sem.at[what, row],
                device_id=(j * LATS + other,),
                device_id_type=MESH,
            )
            for what, (src, dst) in enumerate(((scale, scale_to), (code, code_to)))
        ]

    def owned(j):
        return pl.ds(pl.multiple_of(j * OWNED, 16), OWNED)

    def all_copies(row, code, scale, send_sem, recv_sem):
        return move(row, code, scale, code, scale, send_sem, recv_sem, seats[0])

    for row in range(ROWS):
        if row == 0:
            loads[0].wait()
            loads[1].wait()
        else:
            loads[2].wait()
        part_v[row], part_s[row] = encode(dot3(f_v, x_v[row]))
        if row == 0:
            pl.semaphore_wait(barrier, SEGMENTS)
        for j in seats:
            for copy in move(
                row, part_v.at[row, owned(j)], part_s.at[row], got_v.at[row, seat], got_s.at[row, seat], s1, r1, j
            ):
                copy.start()

    for i in range(3, 9):
        loads[i].wait()
    wi_v[...] = wi_v[...] * jnp.bfloat16(0.5)
    wm_v[...] = wm_v[...] * jnp.bfloat16(0.5)
    for row in range(ROWS):
        for copies in all_copies(row, got_v.at[row], got_s.at[row], s1, r1):
            copies.wait_recv()
        total = decode(got_v[row, 0], got_s[row, 0])
        for j in range(1, SEGMENTS):
            total = total + decode(got_v[row, j], got_s[row, j])
        number = lax.rem(seat, 4) * OWNED + lax.broadcasted_iota(jnp.int32, (OWNED, 1), 0)
        total = jnp.where(number <= cutoffs[other * ROWS + row], total, 0.0)
        sum_v[row], sum_s[row] = encode(total)
        for j in seats:
            for copy in move(
                row, sum_v.at[row], sum_s.at[row], codes[row].at[owned(seat)], scales[row].at[seat], s2, r2, j
            ):
                copy.start()

    for copies in all_copies(0, codes[0], scales[0], s2, r2):
        copies.wait_recv()
    out[...] = finish(0, codes[0], scales[0], i_v, wi_v, wm_v, wo_v, listed)
    for row in range(ROWS):
        for copies in all_copies(row, part_v.at[row], got_s.at[row], s1, r1):
            copies.wait_send()
        for copies in all_copies(row, codes[row], scales[row], s2, r2):
            copies.wait_send()
    for copies in all_copies(1, codes[1], scales[1], s2, r2):
        copies.wait_recv()


def close(first, code_v, scale_v, i_v, wi_v, wm_v, wo_v, listed_h, out, listed, second, sem):
    load = pltpu.make_async_copy(listed_h, listed, sem.at[ROWS])
    load.start()
    store = pltpu.make_async_copy(first, out.at[0, :, 0, :], sem.at[0])
    store.start()
    second[...] = finish(1, code_v, scale_v, i_v, wi_v, wm_v, wo_v, listed, load.wait)
    last = pltpu.make_async_copy(second, out.at[0, :, 1, :], sem.at[1])
    last.start()
    store.wait()
    last.wait()


def local(forward, inverse, state, cutoffs, listed, w_in, w_mid, w_out):
    hbm = pl.BlockSpec(memory_space=pltpu.HBM)
    hidden = w_mid.shape[0]
    f32, bf16, i16 = jnp.float32, jnp.bfloat16, jnp.int16
    dma = pltpu.SemaphoreType.DMA
    vmem = pl.BlockSpec(memory_space=pltpu.VMEM)
    operands = (state.transpose(0, 3, 1, 2), cutoffs, listed, w_in, w_mid, w_out, forward, inverse)
    kept = pl.pallas_call(
        kernel,
        out_shape=[
            pltpu.VMEM((SEG, CHANNELS), f32),
            pltpu.VMEM((COEFS, CHANNELS), i16),
            pltpu.VMEM((SEGMENTS, 1, CHANNELS), f32),
            pltpu.VMEM((SEG, 3 * COEFS), bf16),
            pltpu.VMEM((CHANNELS, hidden), bf16),
            pltpu.VMEM((hidden, hidden), bf16),
            pltpu.VMEM((hidden, CHANNELS), bf16),
        ],
        in_specs=[hbm] * len(operands),
        out_specs=[vmem] * 7,
        scratch_shapes=[
            pltpu.SMEM(cutoffs.shape, jnp.int32),
            pltpu.SMEM(listed.shape, jnp.int32),
            pltpu.VMEM((ROWS, SEG, CHANNELS), f32),
            pltpu.VMEM((2, COEFS, SEG), bf16),
            pltpu.VMEM((ROWS, COEFS, CHANNELS), i16),
            pltpu.VMEM((ROWS, 1, CHANNELS), f32),
            pltpu.VMEM((ROWS, SEGMENTS, OWNED, CHANNELS), i16),
            pltpu.VMEM((ROWS, SEGMENTS, 1, CHANNELS), f32),
            pltpu.VMEM((ROWS, OWNED, CHANNELS), i16),
            pltpu.VMEM((ROWS, 1, CHANNELS), f32),
            pltpu.VMEM((COEFS, CHANNELS), i16),
            pltpu.VMEM((SEGMENTS, 1, CHANNELS), f32),
            dma((9,)),
            dma((2, ROWS)),
            dma((2, ROWS)),
            dma((2, ROWS)),
            dma((2, ROWS)),
        ],
        compiler_params=pltpu.CompilerParams(collective_id=0, has_side_effects=True, vmem_limit_bytes=40 << 20),
        cost_estimate=pl.CostEstimate(flops=2_000_000_000, bytes_accessed=6_000_000, transcendentals=500_000),
    )(*[pltpu.with_memory_space_constraint(array, pltpu.HBM) for array in operands])
    result = pl.pallas_call(
        close,
        out_shape=jax.ShapeDtypeStruct((1, SEG, ROWS, CHANNELS), f32),
        in_specs=[vmem] * 7 + [hbm],
        out_specs=hbm,
        scratch_shapes=[pltpu.SMEM(listed.shape, jnp.int32), pltpu.VMEM((SEG, CHANNELS), f32), dma((ROWS + 1,))],
        compiler_params=pltpu.CompilerParams(vmem_limit_bytes=40 << 20),
        cost_estimate=pl.CostEstimate(flops=1_000_000_000, bytes_accessed=2_000_000, transcendentals=500_000),
    )(*[pltpu.with_memory_space_constraint(array, pltpu.VMEM) for array in kept], pltpu.with_memory_space_constraint(listed, pltpu.HBM))
    return result.transpose(0, 2, 3, 1)


def solution(mesh):
    forward, inverse = tables()

    def whole(prognostic, cutoffs, listed, weight_in, weight_mid, weight_out):
        return local(
            jnp.asarray(forward), jnp.asarray(inverse), prognostic, cutoffs, listed, weight_in, weight_mid, weight_out
        )

    return jax.shard_map(
        whole,
        mesh=mesh,
        in_specs=(P("tiles", None, None, None), P(), P("tiles", None), P(), P(), P()),
        out_specs=P("tiles", None, None, None),
        check_vma=False,
    )
```
